512 devices in a mesh: seq: 64 (over y, z), ch: 8 (over x, core).
Axes of the slice: x: 4, y: 4, z: 16, core: 2. Of those that a mesh axis runs over, the one named last changes fastest.
Arguments:
- gate_query: bfloat16 [2048, 8192], P('ch', 'seq'), may hold values from -6 to 6
- gate_key: bfloat16 [2048, 8192], P('ch', 'seq'), may hold values from -6 to 6
- gate_value: bfloat16 [2048, 8192], P('ch', 'seq'), may hold values from -6 to 6
- filters: float32 [128, 8192], P(None, ('seq', 'ch')), may hold values from -6 to 6
- upstream: bfloat16 [2048, 8192], P('ch', 'seq'), may hold values from -6 to 6
Outputs:
- mixed: bfloat16 [2048, 8192], P('ch', 'seq')
- grad_query: bfloat16 [2048, 8192], P('ch', 'seq')
- grad_key: bfloat16 [2048, 8192], P('ch', 'seq')
- grad_value: bfloat16 [2048, 8192], P('ch', 'seq')
- grad_filters: float32 [128, 8192], P(None, ('seq', 'ch'))
The draws below stay inside these ranges and needn't reach their ends.
All inputs are finite; a program needn't handle non-finite values.
Results may differ from the reference program's by a relative error of at most 0.002.
Values sent between devices are 32-bit elements; how exact they have to be, the bound alone decides.
No kernel may reach another device: no remote copies, remote signals or barrier semaphores. Data moves between devices by JAX's collectives and lax.ppermute only.
A program may use at most 64 MiB of HBM per device.

```python
import math
import jax
import jax.numpy as jnp

GROUP = 16
CHANNELS = 2048
FILTERS = 128
LENGTH = 8192


def levels(key, shape, shards, low, top_value):
    def one(position, parts):
        draws = jax.random.uniform(jax.random.fold_in(jax.random.fold_in(key, 6), position), (parts,), jnp.float32, low / len(shards), top_value / len(shards))
        return jnp.repeat(jnp.exp(draws), shape[position] // parts).reshape((-1,) + (1,) * (len(shape) - position - 1))

    level = one(*shards[0])
    for cut in shards[1:]:
        level = level * one(*cut)
    return level


def centred(own_key, extent, deviation, most, shards=(), kind=jnp.bfloat16):
    array = jax.random.normal(own_key, extent, jnp.float32) * deviation
    if len(shards) > 0:
        array = levels(own_key, extent, shards, -0.22, 0.18) * array
    return jnp.clip(array, min=-most, max=most).astype(kind)


def setup_inputs(seed: int = 0) -> dict:
    seeds = jax.random.split(jax.random.key(seed), 6)
    gate_query = centred(seeds[0], (CHANNELS, LENGTH), 1.0, 6.0, ((0, 8), (1, 64)))
    gate_key = centred(seeds[1], (CHANNELS, LENGTH), 1.0, 6.0, ((0, 8), (1, 64)))
    gate_value = centred(seeds[2], (CHANNELS, LENGTH), 1.0, 6.0, ((0, 8), (1, 64)))
    filters = centred(seeds[3], (FILTERS, LENGTH), 1.0, 6.0, ((1, 512),), jnp.float32)
    upstream = centred(seeds[4], (CHANNELS, LENGTH), 1.0, 6.0, ((0, 8), (1, 64)))
    return dict(gate_query=gate_query, gate_key=gate_key, gate_value=gate_value, filters=filters, upstream=upstream)


def reference(gate_query, gate_key, gate_value, filters, upstream):
    padded_len = 2 * LENGTH
    filter_tap = filters / math.sqrt(LENGTH)
    query_gate = gate_query.astype(jnp.float32)
    key_gate = gate_key.astype(jnp.float32)
    value_gate = gate_value.astype(jnp.float32)
    upstream_f32 = upstream.astype(jnp.float32)
    signal = key_gate * value_gate
    grad_gate = upstream_f32 * query_gate
    spec_signal = jnp.fft.rfft(signal, n=padded_len, axis=-1)
    spec_taps = jnp.repeat(jnp.fft.rfft(filter_tap, n=padded_len, axis=-1), GROUP, axis=0)
    spec_grad = jnp.fft.rfft(grad_gate, n=padded_len, axis=-1)
    mixed_field = jnp.fft.irfft(spec_signal * spec_taps, n=padded_len, axis=-1)[:, :LENGTH]
    grad_signal = jnp.fft.irfft(spec_grad * jnp.conj(spec_taps), n=padded_len, axis=-1)[:, :LENGTH]
    cross_spec = (spec_grad * jnp.conj(spec_signal)).reshape(FILTERS, GROUP, LENGTH + 1).sum(axis=1)
    grad_filters = jnp.fft.irfft(cross_spec, n=padded_len, axis=-1)[:, :LENGTH] / math.sqrt(LENGTH)
    mixed = (query_gate * mixed_field).astype(jnp.bfloat16)
    grad_query = (upstream_f32 * mixed_field).astype(jnp.bfloat16)
    grad_key = (grad_signal * value_gate).astype(jnp.bfloat16)
    grad_value = (grad_signal * key_gate).astype(jnp.bfloat16)
    return (mixed, grad_query, grad_key, grad_value, grad_filters.astype(jnp.float32))
```

```python
import functools
import math

import jax
import jax.numpy as jnp
import ml_dtypes
import numpy as np
from jax import lax
from jax.experimental import pallas as pl
from jax.experimental.pallas import tpu as pltpu
from jax.sharding import PartitionSpec as P

f32 = jnp.float32
bf16 = jnp.bfloat16
vmem = pl.BlockSpec(memory_space=pltpu.VMEM)


def halves(table):
    high = table.astype(ml_dtypes.bfloat16)
    low = (table - high.astype(np.float64)).astype(ml_dtypes.bfloat16)
    return high, low


def make_tables(parts, width):
    total = parts * width
    k1 = np.arange(parts) + 0.25
    p = np.arange(parts)
    b = np.arange(width)
    outer = 2.0 * np.pi / parts * (k1[:, None] * p[None, :])
    first = np.concatenate([np.cos(outer), -np.sin(outer)], axis=0)
    last = np.concatenate([np.cos(outer.T), -np.sin(outer.T)], axis=1) / total
    turn = 2.0 * np.pi / total * (k1[:, None] * b[None, :])
    twiddle = np.concatenate([np.cos(turn), -np.sin(turn)], axis=1).astype(np.float32)
    inner = 2.0 * np.pi / width * (b[:, None] * b[None, :] % width)
    cosine, sine = np.cos(inner), np.sin(inner)
    forward = np.block([[cosine, -sine], [sine, cosine]])
    inverse = np.block([[cosine, sine], [-sine, cosine]])
    first_high, first_low = halves(first)
    last_high, last_low = halves(last)
    return dict(
        first=np.concatenate([first_high, first_high, first_low], axis=1),
        last=np.concatenate([last_high, last_high, last_low], axis=1),
        twiddle=twiddle,
        forward=np.stack(halves(forward)),
        inverse=np.stack(halves(inverse)),
    )


def split(value):
    high = value.astype(bf16)
    return high, (value - high.astype(f32)).astype(bf16)


def dot(left, right):
    return jnp.dot(left, right, preferred_element_type=f32)


def stacked_dot(table, value):
    high, low = split(value)
    return dot(table, jnp.concatenate([high, low, high], axis=0))


def table_dot(value, table_ref):
    high, low = split(value)
    return dot(high, table_ref[0]) + (dot(low, table_ref[0]) + dot(high, table_ref[1]))


def to_spectrum(rows, first_ref, twiddle_ref, forward_ref):
    parts, width = rows[0].shape
    stage = stacked_dot(first_ref[...], jnp.concatenate(rows, axis=1))
    cosine, sine = twiddle_ref[:, :width], twiddle_ref[:, width:]
    turned = []
    for r in range(len(rows)):
        real = stage[:parts, r * width : (r + 1) * width]
        imag = stage[parts:, r * width : (r + 1) * width]
        turned.append(
            jnp.concatenate([real * cosine - imag * sine, real * sine + imag * cosine], axis=1)
        )
    return table_dot(jnp.concatenate(turned, axis=0), forward_ref)


def from_spectrum(spectrum, last_ref, twiddle_ref, inverse_ref):
    parts = last_ref.shape[0]
    width = spectrum.shape[1] // 2
    stage = table_dot(spectrum, inverse_ref)
    cosine, sine = twiddle_ref[:, :width], twiddle_ref[:, width:]
    turned = []
    for r in range(stage.shape[0] // parts):
        real = stage[r * parts : (r + 1) * parts, :width]
        imag = stage[r * parts : (r + 1) * parts, width:]
        turned.append(
            jnp.concatenate([real * cosine + imag * sine, imag * cosine - real * sine], axis=0)
        )
    return stacked_dot(last_ref[...], jnp.concatenate(turned, axis=1))


def times(a, b):
    w = a.shape[1] // 2
    ar, ai, br, bi = a[:, :w], a[:, w:], b[:, :w], b[:, w:]
    return jnp.concatenate([ar * br - ai * bi, ar * bi + ai * br], axis=1)


def times_conj(a, b):
    w = a.shape[1] // 2
    ar, ai, br, bi = a[:, :w], a[:, w:], b[:, :w], b[:, w:]
    return jnp.concatenate([ar * br + ai * bi, ai * br - ar * bi], axis=1)


def lane_blocks(pieces):
    count = len(pieces)
    block = pieces[0].shape[1] // count
    lane = lax.broadcasted_iota(jnp.int32, pieces[0].shape, 1) // block
    out = []
    for c in range(count):
        total = pieces[0] if c == 0 else pltpu.roll(pieces[0], (-c) % count * block, 1)
        for a in range(1, count):
            shift = (a - c) % count * block
            moved = pieces[a] if shift == 0 else pltpu.roll(pieces[a], shift, 1)
            total = jnp.where(lane == a, moved, total)
        out.append(total)
    return out


def gates_kernel(sizes, query_ref, key_ref, value_ref, filters_ref, upstream_ref, out_ref, rows_ref):
    parts, channels, own, groups = sizes
    rows = 2 * own + 1
    filter_count = filters_ref.shape[0] // groups
    share = parts // filter_count
    rows_ref[0] = key_ref[...].astype(f32) * value_ref[...].astype(f32)
    rows_ref[1] = upstream_ref[...].astype(f32) * query_ref[...].astype(f32)
    for which in range(2):
        for j in range(own):
            out_ref[pl.ds(which * own + j, parts, stride=rows), :] = rows_ref[
                which, pl.ds(j, parts, stride=own), :
            ]
    side = jnp.concatenate(
        [filters_ref[g * filter_count : (g + 1) * filter_count, :] for g in range(groups)], axis=1
    )
    for i in range(share):
        out_ref[pl.ds(2 * own + rows * i, filter_count, stride=rows * share), :] = side


def spectra_kernel(
    sizes, x_ref, first_ref, twiddle_ref, forward_ref, inverse_ref, last_ref, spec_ref, out_ref
):
    parts, channels, own, groups = sizes
    rows = 2 * own + 1
    blocks = [x_ref[pl.ds(r, parts, stride=rows), :] for r in range(rows)]
    spectrum = to_spectrum(blocks[: 2 * own], first_ref, twiddle_ref, forward_ref)
    spec_ref[...] = spectrum
    cross = None
    for j in range(own):
        term = times_conj(
            spectrum[(own + j) * parts : (own + j + 1) * parts],
            spectrum[j * parts : (j + 1) * parts],
        )
        cross = term if cross is None else cross + term
    grad_taps = from_spectrum(cross, last_ref, twiddle_ref, inverse_ref)
    for which, block in enumerate((blocks[2 * own], grad_taps)):
        count = parts // groups
        pieces = lane_blocks([block[a * count : (a + 1) * count] for a in range(groups)])
        for g in range(groups):
            out_ref[g, which * count : (which + 1) * count, :] = pieces[g]


def fields_kernel(
    sizes, tap_scale, spec_ref, side_ref, first_ref, twiddle_ref, forward_ref, inverse_ref, last_ref, out_ref
):
    parts, channels, own, groups = sizes
    rows = 2 * own + 1
    count = parts // groups
    taps, grad_taps = (
        jnp.concatenate(
            lane_blocks([side_ref[g, which * count : (which + 1) * count, :] for g in range(groups)]),
            axis=0,
        )
        for which in range(2)
    )
    out_ref[pl.ds(2 * own, parts, stride=rows), :] = grad_taps * tap_scale
    taps = to_spectrum([taps * tap_scale], first_ref, twiddle_ref, forward_ref)
    products = []
    for j in range(own):
        products.append(times(spec_ref[j * parts : (j + 1) * parts, :], taps))
    for j in range(own, 2 * own):
        products.append(times_conj(spec_ref[j * parts : (j + 1) * parts, :], taps))
    fields = from_spectrum(jnp.concatenate(products, axis=0), last_ref, twiddle_ref, inverse_ref)
    width = fields.shape[1] // (2 * own)
    for r in range(2 * own):
        out_ref[pl.ds(r, parts, stride=rows), :] = fields[:, r * width : (r + 1) * width]


def outputs_kernel(
    sizes,
    y_ref,
    query_ref,
    key_ref,
    value_ref,
    upstream_ref,
    mixed_ref,
    grad_query_ref,
    grad_key_ref,
    grad_value_ref,
    grad_filters_ref,
    rows_ref,
):
    parts, channels, own, groups = sizes
    rows = 2 * own + 1
    filter_count = grad_filters_ref.shape[0] // groups
    share = parts // filter_count
    for which in range(2):
        for j in range(own):
            rows_ref[which, pl.ds(j, parts, stride=own), :] = y_ref[
                pl.ds(which * own + j, parts, stride=rows), :
            ]
    mixed_field = rows_ref[0]
    grad_signal = rows_ref[1]
    mixed_ref[...] = (query_ref[...].astype(f32) * mixed_field).astype(bf16)
    grad_query_ref[...] = (upstream_ref[...].astype(f32) * mixed_field).astype(bf16)
    grad_key_ref[...] = (grad_signal * value_ref[...].astype(f32)).astype(bf16)
    grad_value_ref[...] = (grad_signal * key_ref[...].astype(f32)).astype(bf16)
    side = None
    for i in range(share):
        term = y_ref[pl.ds(2 * own + rows * i, filter_count, stride=rows * share), :]
        side = term if side is None else side + term
    block = side.shape[1] // groups
    for g in range(groups):
        grad_filters_ref[g * filter_count : (g + 1) * filter_count, :] = side[
            :, g * block : (g + 1) * block
        ]


def call(kernel, out_shape, scratch=()):
    return pl.pallas_call(
        kernel,
        out_shape=out_shape,
        out_specs=jax.tree.map(lambda _: vmem, out_shape),
        scratch_shapes=scratch,
        compiler_params=pltpu.CompilerParams(vmem_limit_bytes=32 * 1024 * 1024),
    )


def shards(gate_query, gate_key, gate_value, filters, upstream):
    channels, width = gate_value.shape
    parts = lax.axis_size("seq")
    groups = lax.axis_size("ch")
    own = channels // parts
    rows = 2 * own + 1
    sizes = (parts, channels, own, groups)
    tap_scale = 1.0 / math.sqrt(parts * width)
    tables = make_tables(parts, width)
    first, twiddle, forward, inverse, last = (
        jnp.asarray(tables[name]) for name in ("first", "twiddle", "forward", "inverse", "last")
    )

    def exchange(block):
        block = block.reshape(parts, rows, 1, width)
        block = lax.all_to_all(block, "seq", split_axis=0, concat_axis=0, tiled=True)
        return block.reshape(parts * rows, width)

    shape = jax.ShapeDtypeStruct
    packed = call(
        functools.partial(gates_kernel, sizes),
        shape((parts * rows, width), f32),
        [pltpu.VMEM((2, channels, width), f32)],
    )(gate_query, gate_key, gate_value, filters, upstream)
    packed = exchange(packed)
    spectra, side = call(
        functools.partial(spectra_kernel, sizes),
        (
            shape((2 * own * parts, 2 * width), f32),
            shape((groups, 2 * parts // groups, width), f32),
        ),
    )(packed, first, twiddle, forward, inverse, last)
    side = lax.all_to_all(side, "ch", split_axis=0, concat_axis=0, tiled=True)
    packed = call(functools.partial(fields_kernel, sizes, tap_scale), shape((parts * rows, width), f32))(
        spectra, side, first, twiddle, forward, inverse, last
    )
    packed = exchange(packed)
    gates = shape((channels, width), bf16)
    return call(
        functools.partial(outputs_kernel, sizes),
        (gates, gates, gates, gates, shape(filters.shape, f32)),
        [pltpu.VMEM((2, channels, width), f32)],
    )(packed, gate_query, gate_key, gate_value, upstream)


def solution(mesh):
    in_specs = (
        P("ch", "seq"),
        P("ch", "seq"),
        P("ch", "seq"),
        P(None, ("seq", "ch")),
        P("ch", "seq"),
    )
    out_specs = (
        P("ch", "seq"),
        P("ch", "seq"),
        P("ch", "seq"),
        P("ch", "seq"),
        P(None, ("seq", "ch")),
    )
    return jax.shard_map(shards, mesh=mesh, in_specs=in_specs, out_specs=out_specs, check_vma=False)
```

```python
import functools
import math

import jax
import jax.numpy as jnp
import ml_dtypes
import numpy as np
from jax import lax
from jax.experimental import pallas as pl
from jax.experimental.pallas import tpu as pltpu
from jax.sharding import PartitionSpec as P

f32 = jnp.float32
bf16 = jnp.bfloat16
vmem = pl.BlockSpec(memory_space=pltpu.VMEM)


def halves(table):
    high = table.astype(ml_dtypes.bfloat16)
    low = (table - high.astype(np.float64)).astype(ml_dtypes.bfloat16)
    return high, low


def make_tables(parts, width):
    total = parts * width
    k1 = np.arange(parts) + 0.25
    p = np.arange(parts)
    b = np.arange(width)
    outer = 2.0 * np.pi / parts * (k1[:, None] * p[None, :])
    first = np.concatenate([np.cos(outer), -np.sin(outer)], axis=0)
    last = np.concatenate([np.cos(outer.T), -np.sin(outer.T)], axis=1) / total
    turn = 2.0 * np.pi / total * (k1[:, None] * b[None, :])
    twiddle = np.concatenate([np.cos(turn), -np.sin(turn)], axis=1).astype(np.float32)
    inner = 2.0 * np.pi / width * (b[:, None] * b[None, :] % width)
    cosine, sine = np.cos(inner), np.sin(inner)
    forward = np.block([[cosine, -sine], [sine, cosine]])
    inverse = np.block([[cosine, sine], [-sine, cosine]])
    first_high, first_low = halves(first)
    last_high, last_low = halves(last)
    return dict(
        first=np.concatenate([first_high, first_high, first_low], axis=1),
        last=np.concatenate([last_high, last_high, last_low], axis=1),
        twiddle=twiddle,
        forward=np.stack(halves(forward)),
        inverse=np.stack(halves(inverse)),
    )


def split(value):
    high = value.astype(bf16)
    return high, (value - high.astype(f32)).astype(bf16)


def dot(left, right):
    return jnp.dot(left, right, preferred_element_type=f32)


def stacked_dot(table, value):
    high, low = split(value)
    return dot(table, jnp.concatenate([high, low, high], axis=0))


def table_dot(value, table_ref):
    high, low = split(value)
    return dot(high, table_ref[0]) + (dot(low, table_ref[0]) + dot(high, table_ref[1]))


def to_spectrum(rows, first_ref, twiddle_ref, forward_ref):
    parts, width = rows[0].shape
    stage = stacked_dot(first_ref[...], jnp.concatenate(rows, axis=1))
    cosine, sine = twiddle_ref[:, :width], twiddle_ref[:, width:]
    turned = []
    for r in range(len(rows)):
        real = stage[:parts, r * width : (r + 1) * width]
        imag = stage[parts:, r * width : (r + 1) * width]
        turned.append(
            jnp.concatenate([real * cosine - imag * sine, real * sine + imag * cosine], axis=1)
        )
    return table_dot(jnp.concatenate(turned, axis=0), forward_ref)


def from_spectrum(spectrum, last_ref, twiddle_ref, inverse_ref):
    parts = last_ref.shape[0]
    width = spectrum.shape[1] // 2
    stage = table_dot(spectrum, inverse_ref)
    cosine, sine = twiddle_ref[:, :width], twiddle_ref[:, width:]
    turned = []
    for r in range(stage.shape[0] // parts):
        real = stage[r * parts : (r + 1) * parts, :width]
        imag = stage[r * parts : (r + 1) * parts, width:]
        turned.append(
            jnp.concatenate([real * cosine + imag * sine, imag * cosine - real * sine], axis=0)
        )
    return stacked_dot(last_ref[...], jnp.concatenate(turned, axis=1))


def times(a, b):
    w = a.shape[1] // 2
    ar, ai, br, bi = a[:, :w], a[:, w:], b[:, :w], b[:, w:]
    return jnp.concatenate([ar * br - ai * bi, ar * bi + ai * br], axis=1)


def times_conj(a, b):
    w = a.shape[1] // 2
    ar, ai, br, bi = a[:, :w], a[:, w:], b[:, :w], b[:, w:]
    return jnp.concatenate([ar * br + ai * bi, ai * br - ar * bi], axis=1)


def lane_blocks(pieces):
    count = len(pieces)
    block = pieces[0].shape[1] // count
    lane = lax.broadcasted_iota(jnp.int32, pieces[0].shape, 1) // block
    out = []
    for c in range(count):
        total = pieces[0] if c == 0 else pltpu.roll(pieces[0], (-c) % count * block, 1)
        for a in range(1, count):
            shift = (a - c) % count * block
            moved = pieces[a] if shift == 0 else pltpu.roll(pieces[a], shift, 1)
            total = jnp.where(lane == a, moved, total)
        out.append(total)
    return out


def gates_kernel(
    sizes,
    query_hbm,
    key_hbm,
    value_hbm,
    upstream_hbm,
    filters_hbm,
    out_ref,
    gates_ref,
    filters_ref,
    rows_ref,
    sems,
):
    parts, channels, own, groups = sizes
    rows = 2 * own + 1
    filter_count = filters_ref.shape[1] // groups
    share = parts // filter_count
    loads = [pltpu.make_async_copy(filters_hbm, filters_ref, sems.at[4])]
    for i, source in enumerate((key_hbm, value_hbm, upstream_hbm, query_hbm)):
        loads.append(pltpu.make_async_copy(source, gates_ref.at[i], sems.at[i]))
    for load in loads:
        load.start()
    loads[0].wait()
    taps = filters_ref[...].T
    side = jnp.concatenate(
        [taps[g * filter_count : (g + 1) * filter_count, :] for g in range(groups)], axis=1
    )
    for i in range(share):
        out_ref[pl.ds(2 * own + rows * i, filter_count, stride=rows * share), :] = side
    for which in range(2):
        loads[1 + 2 * which].wait()
        loads[2 + 2 * which].wait()
        rows_ref[which] = gates_ref[2 * which].astype(f32) * gates_ref[2 * which + 1].astype(f32)
        for j in range(own):
            out_ref[pl.ds(which * own + j, parts, stride=rows), :] = rows_ref[
                which, pl.ds(j, parts, stride=own), :
            ]


def spectra_kernel(
    sizes, x_ref, first_ref, twiddle_ref, forward_ref, inverse_ref, last_ref, spec_ref, out_ref
):
    parts, channels, own, groups = sizes
    rows = 2 * own + 1
    blocks = [x_ref[pl.ds(r, parts, stride=rows), :] for r in range(rows)]
    spectrum = to_spectrum(blocks[: 2 * own], first_ref, twiddle_ref, forward_ref)
    spec_ref[...] = spectrum
    cross = None
    for j in range(own):
        term = times_conj(
            spectrum[(own + j) * parts : (own + j + 1) * parts],
            spectrum[j * parts : (j + 1) * parts],
        )
        cross = term if cross is None else cross + term
    grad_taps = from_spectrum(cross, last_ref, twiddle_ref, inverse_ref)
    for which, block in enumerate((blocks[2 * own], grad_taps)):
        count = parts // groups
        pieces = lane_blocks([block[a * count : (a + 1) * count] for a in range(groups)])
        for g in range(groups):
            out_ref[g, which * count : (which + 1) * count, :] = pieces[g]


def fields_kernel(
    sizes, tap_scale, spec_ref, side_ref, first_ref, twiddle_ref, forward_ref, inverse_ref, last_ref, out_ref
):
    parts, channels, own, groups = sizes
    rows = 2 * own + 1
    count = parts // groups
    taps, grad_taps = (
        jnp.concatenate(
            lane_blocks([side_ref[g, which * count : (which + 1) * count, :] for g in range(groups)]),
            axis=0,
        )
        for which in range(2)
    )
    out_ref[pl.ds(2 * own, parts, stride=rows), :] = grad_taps * tap_scale
    taps = to_spectrum([taps * tap_scale], first_ref, twiddle_ref, forward_ref)
    products = []
    for j in range(own):
        products.append(times(spec_ref[j * parts : (j + 1) * parts, :], taps))
    for j in range(own, 2 * own):
        products.append(times_conj(spec_ref[j * parts : (j + 1) * parts, :], taps))
    fields = from_spectrum(jnp.concatenate(products, axis=0), last_ref, twiddle_ref, inverse_ref)
    width = fields.shape[1] // (2 * own)
    for r in range(2 * own):
        out_ref[pl.ds(r, parts, stride=rows), :] = fields[:, r * width : (r + 1) * width]


def outputs_kernel(
    sizes,
    y_ref,
    query_ref,
    key_ref,
    value_ref,
    upstream_ref,
    mixed_ref,
    grad_query_ref,
    grad_key_ref,
    grad_value_ref,
    grad_filters_ref,
    rows_ref,
):
    parts, channels, own, groups = sizes
    rows = 2 * own + 1
    filter_count = grad_filters_ref.shape[1] // groups
    share = parts // filter_count
    for which in range(2):
        for j in range(own):
            rows_ref[which, pl.ds(j, parts, stride=own), :] = y_ref[
                pl.ds(which * own + j, parts, stride=rows), :
            ]
    mixed_field = rows_ref[0]
    grad_signal = rows_ref[1]
    mixed_ref[...] = (query_ref[...].astype(f32) * mixed_field).astype(bf16)
    grad_query_ref[...] = (upstream_ref[...].astype(f32) * mixed_field).astype(bf16)
    grad_key_ref[...] = (grad_signal * value_ref[...].astype(f32)).astype(bf16)
    grad_value_ref[...] = (grad_signal * key_ref[...].astype(f32)).astype(bf16)
    side = None
    for i in range(share):
        term = y_ref[pl.ds(2 * own + rows * i, filter_count, stride=rows * share), :]
        side = term if side is None else side + term
    block = side.shape[1] // groups
    grad_filters_ref[...] = jnp.concatenate(
        [side[:, g * block : (g + 1) * block] for g in range(groups)], axis=0
    ).T


def call(kernel, out_shape, scratch=(), grant=32, **specs):
    return pl.pallas_call(
        kernel,
        out_shape=out_shape,
        out_specs=jax.tree.map(lambda _: vmem, out_shape),
        scratch_shapes=scratch,
        **specs,
        compiler_params=pltpu.CompilerParams(vmem_limit_bytes=grant * 1024 * 1024),
    )


def shards(gate_query, gate_key, gate_value, filters, upstream):
    channels, width = gate_value.shape
    parts = lax.axis_size("seq")
    groups = lax.axis_size("ch")
    own = channels // parts
    rows = 2 * own + 1
    sizes = (parts, channels, own, groups)
    tap_scale = 1.0 / math.sqrt(parts * width)
    tables = make_tables(parts, width)
    first, twiddle, forward, inverse, last = (
        jnp.asarray(tables[name]) for name in ("first", "twiddle", "forward", "inverse", "last")
    )

    def exchange(block):
        block = block.reshape(parts, rows, 1, width)
        block = lax.all_to_all(block, "seq", split_axis=0, concat_axis=0, tiled=True)
        return block.reshape(parts * rows, width)

    shape = jax.ShapeDtypeStruct
    packed = call(
        functools.partial(gates_kernel, sizes),
        shape((parts * rows, width), f32),
        [
            pltpu.VMEM((4, channels, width), bf16),
            pltpu.VMEM(filters.shape[::-1], f32),
            pltpu.VMEM((2, channels, width), f32),
            pltpu.SemaphoreType.DMA((5,)),
        ],
        grant=62,
        in_specs=[pl.BlockSpec(memory_space=pl.ANY)] * 5,
    )(gate_query, gate_key, gate_value, upstream, filters.T)
    packed = exchange(packed)
    spectra, side = call(
        functools.partial(spectra_kernel, sizes),
        (
            shape((2 * own * parts, 2 * width), f32),
            shape((groups, 2 * parts // groups, width), f32),
        ),
    )(packed, first, twiddle, forward, inverse, last)
    side = lax.all_to_all(side, "ch", split_axis=0, concat_axis=0, tiled=True)
    packed = call(functools.partial(fields_kernel, sizes, tap_scale), shape((parts * rows, width), f32))(
        spectra, side, first, twiddle, forward, inverse, last
    )
    packed = exchange(packed)
    gates = shape((channels, width), bf16)
    *grads, grad_filters = call(
        functools.partial(outputs_kernel, sizes),
        (gates, gates, gates, gates, shape(filters.shape[::-1], f32)),
        [pltpu.VMEM((2, channels, width), f32)],
    )(packed, gate_query, gate_key, gate_value, upstream)
    return (*grads, grad_filters.T)


def solution(mesh):
    in_specs = (
        P("ch", "seq"),
        P("ch", "seq"),
        P("ch", "seq"),
        P(None, ("seq", "ch")),
        P("ch", "seq"),
    )
    out_specs = (
        P("ch", "seq"),
        P("ch", "seq"),
        P("ch", "seq"),
        P("ch", "seq"),
        P(None, ("seq", "ch")),
    )
    return jax.shard_map(shards, mesh=mesh, in_specs=in_specs, out_specs=out_specs, check_vma=False)
```

```python
import functools
import math

import jax
import jax.numpy as jnp
import ml_dtypes
import numpy as np
from jax import lax
from jax.experimental import pallas as pl
from jax.experimental.pallas import tpu as pltpu
from jax.sharding import PartitionSpec as P

f32 = jnp.float32
bf16 = jnp.bfloat16
vmem = pl.BlockSpec(memory_space=pltpu.VMEM)


def halves(table):
    high = table.astype(ml_dtypes.bfloat16)
    low = (table - high.astype(np.float64)).astype(ml_dtypes.bfloat16)
    return high, low


def make_tables(parts, width):
    total = parts * width
    k1 = np.arange(parts) + 0.25
    p = np.arange(parts)
    b = np.arange(width)
    outer = 2.0 * np.pi / parts * (k1[:, None] * p[None, :])
    first = np.concatenate([np.cos(outer), -np.sin(outer)], axis=0)
    last = np.concatenate([np.cos(outer.T), -np.sin(outer.T)], axis=1) / total
    turn = 2.0 * np.pi / total * (k1[:, None] * b[None, :])
    twiddle = np.concatenate([np.cos(turn), -np.sin(turn)], axis=1).astype(np.float32)
    inner = 2.0 * np.pi / width * (b[:, None] * b[None, :] % width)
    cosine, sine = np.cos(inner), np.sin(inner)
    forward = np.block([[cosine, -sine], [sine, cosine]])
    inverse = np.block([[cosine, sine], [-sine, cosine]])
    first_high, first_low = halves(first)
    last_high, last_low = halves(last)
    return dict(
        first=np.concatenate([first_high, first_high, first_low], axis=1),
        last=np.concatenate([last_high, last_high, last_low], axis=1),
        twiddle=twiddle,
        forward=np.stack(halves(forward)),
        inverse=np.stack(halves(inverse)),
    )


def split(value):
    high = value.astype(bf16)
    return high, (value - high.astype(f32)).astype(bf16)


def dot(left, right):
    return jnp.dot(left, right, preferred_element_type=f32)


def stacked_dot(table, value):
    high, low = split(value)
    return dot(table, jnp.concatenate([high, low, high], axis=0))


def table_dot(value, table_ref):
    high, low = split(value)
    return dot(high, table_ref[0]) + (dot(low, table_ref[0]) + dot(high, table_ref[1]))


def to_spectrum(rows, first_ref, twiddle_ref, forward_ref):
    parts, width = rows[0].shape
    stage = stacked_dot(first_ref[...], jnp.concatenate(rows, axis=1))
    cosine, sine = twiddle_ref[:, :width], twiddle_ref[:, width:]
    turned = []
    for r in range(len(rows)):
        real = stage[:parts, r * width : (r + 1) * width]
        imag = stage[parts:, r * width : (r + 1) * width]
        turned.append(
            jnp.concatenate([real * cosine - imag * sine, real * sine + imag * cosine], axis=1)
        )
    return table_dot(jnp.concatenate(turned, axis=0), forward_ref)


def from_spectrum(spectrum, last_ref, twiddle_ref, inverse_ref):
    parts = last_ref.shape[0]
    width = spectrum.shape[1] // 2
    stage = table_dot(spectrum, inverse_ref)
    cosine, sine = twiddle_ref[:, :width], twiddle_ref[:, width:]
    turned = []
    for r in range(stage.shape[0] // parts):
        real = stage[r * parts : (r + 1) * parts, :width]
        imag = stage[r * parts : (r + 1) * parts, width:]
        turned.append(
            jnp.concatenate([real * cosine + imag * sine, imag * cosine - real * sine], axis=0)
        )
    return stacked_dot(last_ref[...], jnp.concatenate(turned, axis=1))


def times(a, b):
    w = a.shape[1] // 2
    ar, ai, br, bi = a[:, :w], a[:, w:], b[:, :w], b[:, w:]
    return jnp.concatenate([ar * br - ai * bi, ar * bi + ai * br], axis=1)


def times_conj(a, b):
    w = a.shape[1] // 2
    ar, ai, br, bi = a[:, :w], a[:, w:], b[:, :w], b[:, w:]
    return jnp.concatenate([ar * br + ai * bi, ai * br - ar * bi], axis=1)


def lane_blocks(pieces):
    count = len(pieces)
    block = pieces[0].shape[1] // count
    lane = lax.broadcasted_iota(jnp.int32, pieces[0].shape, 1) // block
    out = []
    for c in range(count):
        total = pieces[0] if c == 0 else pltpu.roll(pieces[0], (-c) % count * block, 1)
        for a in range(1, count):
            shift = (a - c) % count * block
            moved = pieces[a] if shift == 0 else pltpu.roll(pieces[a], shift, 1)
            total = jnp.where(lane == a, moved, total)
        out.append(total)
    return out


def gates_kernel(sizes, signal_ref, grad_ref, filters_ref, out_ref):
    parts, channels, own, groups = sizes
    rows = 2 * own + 1
    filter_count = filters_ref.shape[1] // groups
    share = parts // filter_count
    for which, source in enumerate((signal_ref, grad_ref)):
        for j in range(own):
            out_ref[pl.ds(which * own + j, parts, stride=rows), :] = source[
                pl.ds(j, parts, stride=own), :
            ]
    taps = filters_ref[...].T
    side = jnp.concatenate(
        [taps[g * filter_count : (g + 1) * filter_count, :] for g in range(groups)], axis=1
    )
    for i in range(share):
        out_ref[pl.ds(2 * own + rows * i, filter_count, stride=rows * share), :] = side


def spectra_kernel(
    sizes, x_ref, first_ref, twiddle_ref, forward_ref, inverse_ref, last_ref, spec_ref, out_ref
):
    parts, channels, own, groups = sizes
    rows = 2 * own + 1
    blocks = [x_ref[pl.ds(r, parts, stride=rows), :] for r in range(rows)]
    spectrum = to_spectrum(blocks[: 2 * own], first_ref, twiddle_ref, forward_ref)
    spec_ref[...] = spectrum
    cross = None
    for j in range(own):
        term = times_conj(
            spectrum[(own + j) * parts : (own + j + 1) * parts],
            spectrum[j * parts : (j + 1) * parts],
        )
        cross = term if cross is None else cross + term
    grad_taps = from_spectrum(cross, last_ref, twiddle_ref, inverse_ref)
    for which, block in enumerate((blocks[2 * own], grad_taps)):
        count = parts // groups
        pieces = lane_blocks([block[a * count : (a + 1) * count] for a in range(groups)])
        for g in range(groups):
            out_ref[g, which * count : (which + 1) * count, :] = pieces[g]


def fields_kernel(
    sizes, tap_scale, spec_ref, side_ref, first_ref, twiddle_ref, forward_ref, inverse_ref, last_ref, out_ref
):
    parts, channels, own, groups = sizes
    rows = 2 * own + 1
    count = parts // groups
    taps, grad_taps = (
        jnp.concatenate(
            lane_blocks([side_ref[g, which * count : (which + 1) * count, :] for g in range(groups)]),
            axis=0,
        )
        for which in range(2)
    )
    out_ref[pl.ds(2 * own, parts, stride=rows), :] = grad_taps * tap_scale
    taps = to_spectrum([taps * tap_scale], first_ref, twiddle_ref, forward_ref)
    products = []
    for j in range(own):
        products.append(times(spec_ref[j * parts : (j + 1) * parts, :], taps))
    for j in range(own, 2 * own):
        products.append(times_conj(spec_ref[j * parts : (j + 1) * parts, :], taps))
    fields = from_spectrum(jnp.concatenate(products, axis=0), last_ref, twiddle_ref, inverse_ref)
    width = fields.shape[1] // (2 * own)
    for r in range(2 * own):
        out_ref[pl.ds(r, parts, stride=rows), :] = fields[:, r * width : (r + 1) * width]


def outputs_kernel(
    sizes,
    y_ref,
    query_ref,
    key_ref,
    value_ref,
    upstream_ref,
    mixed_ref,
    grad_query_ref,
    grad_key_ref,
    grad_value_ref,
    grad_filters_ref,
    rows_ref,
):
    parts, channels, own, groups = sizes
    rows = 2 * own + 1
    filter_count = grad_filters_ref.shape[1] // groups
    share = parts // filter_count
    for which in range(2):
        for j in range(own):
            rows_ref[which, pl.ds(j, parts, stride=own), :] = y_ref[
                pl.ds(which * own + j, parts, stride=rows), :
            ]
    mixed_field = rows_ref[0]
    grad_signal = rows_ref[1]
    mixed_ref[...] = (query_ref[...].astype(f32) * mixed_field).astype(bf16)
    grad_query_ref[...] = (upstream_ref[...].astype(f32) * mixed_field).astype(bf16)
    grad_key_ref[...] = (grad_signal * value_ref[...].astype(f32)).astype(bf16)
    grad_value_ref[...] = (grad_signal * key_ref[...].astype(f32)).astype(bf16)
    side = None
    for i in range(share):
        term = y_ref[pl.ds(2 * own + rows * i, filter_count, stride=rows * share), :]
        side = term if side is None else side + term
    block = side.shape[1] // groups
    grad_filters_ref[...] = jnp.concatenate(
        [side[:, g * block : (g + 1) * block] for g in range(groups)], axis=0
    ).T


def call(kernel, out_shape, scratch=(), grant=32, **specs):
    return pl.pallas_call(
        kernel,
        out_shape=out_shape,
        out_specs=jax.tree.map(lambda _: vmem, out_shape),
        scratch_shapes=scratch,
        **specs,
        compiler_params=pltpu.CompilerParams(vmem_limit_bytes=grant * 1024 * 1024),
    )


def shards(gate_query, gate_key, gate_value, filters, upstream):
    channels, width = gate_value.shape
    parts = lax.axis_size("seq")
    groups = lax.axis_size("ch")
    own = channels // parts
    rows = 2 * own + 1
    sizes = (parts, channels, own, groups)
    tap_scale = 1.0 / math.sqrt(parts * width)
    tables = make_tables(parts, width)
    first, twiddle, forward, inverse, last = (
        jnp.asarray(tables[name]) for name in ("first", "twiddle", "forward", "inverse", "last")
    )

    def exchange(block):
        block = block.reshape(parts, rows, 1, width)
        block = lax.all_to_all(block, "seq", split_axis=0, concat_axis=0, tiled=True)
        return block.reshape(parts * rows, width)

    shape = jax.ShapeDtypeStruct
    signal = gate_key.astype(f32) * gate_value.astype(f32)
    grad_gate = upstream.astype(f32) * gate_query.astype(f32)
    packed = call(functools.partial(gates_kernel, sizes), shape((parts * rows, width), f32))(
        signal, grad_gate, filters.T
    )
    packed = exchange(packed)
    spectra, side = call(
        functools.partial(spectra_kernel, sizes),
        (
            shape((2 * own * parts, 2 * width), f32),
            shape((groups, 2 * parts // groups, width), f32),
        ),
    )(packed, first, twiddle, forward, inverse, last)
    side = lax.all_to_all(side, "ch", split_axis=0, concat_axis=0, tiled=True)
    packed = call(functools.partial(fields_kernel, sizes, tap_scale), shape((parts * rows, width), f32))(
        spectra, side, first, twiddle, forward, inverse, last
    )
    packed = exchange(packed)
    gates = shape((channels, width), bf16)
    *grads, grad_filters = call(
        functools.partial(outputs_kernel, sizes),
        (gates, gates, gates, gates, shape(filters.shape[::-1], f32)),
        [pltpu.VMEM((2, channels, width), f32)],
    )(packed, gate_query, gate_key, gate_value, upstream)
    return (*grads, grad_filters.T)


def solution(mesh):
    in_specs = (
        P("ch", "seq"),
        P("ch", "seq"),
        P("ch", "seq"),
        P(None, ("seq", "ch")),
        P("ch", "seq"),
    )
    out_specs = (
        P("ch", "seq"),
        P("ch", "seq"),
        P("ch", "seq"),
        P("ch", "seq"),
        P(None, ("seq", "ch")),
    )
    return jax.shard_map(shards, mesh=mesh, in_specs=in_specs, out_specs=out_specs, check_vma=False)
```

```python
import functools
import math

import jax
import jax.numpy as jnp
import ml_dtypes
import numpy as np
from jax import lax
from jax.experimental import pallas as pl
from jax.experimental.pallas import tpu as pltpu
from jax.sharding import PartitionSpec as P

f32 = jnp.float32
bf16 = jnp.bfloat16
vmem = pl.BlockSpec(memory_space=pltpu.VMEM)


def halves(table):
    high = table.astype(ml_dtypes.bfloat16)
    low = (table - high.astype(np.float64)).astype(ml_dtypes.bfloat16)
    return high, low


def make_tables(parts, width, order):
    total = parts * width
    k1 = np.arange(parts) + 0.25
    p = np.asarray(order)
    b = np.arange(width)
    outer = 2.0 * np.pi / parts * (k1[:, None] * p[None, :])
    first = np.concatenate([np.cos(outer), -np.sin(outer)], axis=0)
    last = np.concatenate([np.cos(outer.T), -np.sin(outer.T)], axis=1) / total
    turn = 2.0 * np.pi / total * (k1[:, None] * b[None, :])
    twiddle = np.concatenate([np.cos(turn), -np.sin(turn)], axis=1).astype(np.float32)
    inner = 2.0 * np.pi / width * (b[:, None] * b[None, :] % width)
    cosine, sine = np.cos(inner), np.sin(inner)
    forward = np.block([[cosine, -sine], [sine, cosine]])
    inverse = np.block([[cosine, sine], [-sine, cosine]])
    first_high, first_low = halves(first)
    last_high, last_low = halves(last)
    return dict(
        first=np.concatenate([first_high, first_high, first_low], axis=1),
        last=np.concatenate([last_high, last_high, last_low], axis=1),
        twiddle=twiddle,
        forward=np.stack(halves(forward)),
        inverse=np.stack(halves(inverse)),
    )


def split(value):
    high = value.astype(bf16)
    return high, (value - high.astype(f32)).astype(bf16)


def dot(left, right):
    return jnp.dot(left, right, preferred_element_type=f32)


def stacked_dot(table, value):
    high, low = split(value)
    return dot(table, jnp.concatenate([high, low, high], axis=0))


def table_dot(value, table_ref):
    high, low = split(value)
    return dot(high, table_ref[0]) + (dot(low, table_ref[0]) + dot(high, table_ref[1]))


def to_spectrum(rows, first_ref, twiddle_ref, forward_ref):
    parts, width = rows[0].shape
    stage = stacked_dot(first_ref[...], jnp.concatenate(rows, axis=1))
    cosine, sine = twiddle_ref[:, :width], twiddle_ref[:, width:]
    turned = []
    for r in range(len(rows)):
        real = stage[:parts, r * width : (r + 1) * width]
        imag = stage[parts:, r * width : (r + 1) * width]
        turned.append(
            jnp.concatenate([real * cosine - imag * sine, real * sine + imag * cosine], axis=1)
        )
    return table_dot(jnp.concatenate(turned, axis=0), forward_ref)


def from_spectrum(spectrum, last_ref, twiddle_ref, inverse_ref):
    parts = last_ref.shape[0]
    width = spectrum.shape[1] // 2
    stage = table_dot(spectrum, inverse_ref)
    cosine, sine = twiddle_ref[:, :width], twiddle_ref[:, width:]
    turned = []
    for r in range(stage.shape[0] // parts):
        real = stage[r * parts : (r + 1) * parts, :width]
        imag = stage[r * parts : (r + 1) * parts, width:]
        turned.append(
            jnp.concatenate([real * cosine + imag * sine, imag * cosine - real * sine], axis=0)
        )
    return stacked_dot(last_ref[...], jnp.concatenate(turned, axis=1))


def times(a, b):
    w = a.shape[1] // 2
    ar, ai, br, bi = a[:, :w], a[:, w:], b[:, :w], b[:, w:]
    return jnp.concatenate([ar * br - ai * bi, ar * bi + ai * br], axis=1)


def times_conj(a, b):
    w = a.shape[1] // 2
    ar, ai, br, bi = a[:, :w], a[:, w:], b[:, :w], b[:, w:]
    return jnp.concatenate([ar * br + ai * bi, ai * br - ar * bi], axis=1)


def lane_blocks(pieces):
    count = len(pieces)
    block = pieces[0].shape[1] // count
    lane = lax.broadcasted_iota(jnp.int32, pieces[0].shape, 1) // block
    out = []
    for c in range(count):
        total = pieces[0] if c == 0 else pltpu.roll(pieces[0], (-c) % count * block, 1)
        for a in range(1, count):
            shift = (a - c) % count * block
            moved = pieces[a] if shift == 0 else pltpu.roll(pieces[a], shift, 1)
            total = jnp.where(lane == a, moved, total)
        out.append(total)
    return out


def gates_kernel(sizes, signal_ref, grad_ref, filters_ref, out_ref):
    parts, channels, own, groups = sizes
    rows = 2 * own + 1
    filter_count = filters_ref.shape[1] // groups
    share = parts // filter_count
    for which, source in enumerate((signal_ref, grad_ref)):
        for j in range(own):
            out_ref[pl.ds(which * own + j, parts, stride=rows), :] = source[
                pl.ds(j, parts, stride=own), :
            ]
    taps = filters_ref[...].T
    side = jnp.concatenate(
        [taps[g * filter_count : (g + 1) * filter_count, :] for g in range(groups)], axis=1
    )
    for i in range(share):
        out_ref[pl.ds(2 * own + rows * i, filter_count, stride=rows * share), :] = side


def spectra_kernel(
    sizes, members, x_ref, first_ref, twiddle_ref, forward_ref, inverse_ref, last_ref, spec_ref, out_ref
):
    parts, channels, own, groups = sizes
    rows = 2 * own + 1
    blocks = [x_ref[pl.ds(r, parts, stride=rows), :] for r in range(rows)]
    spectrum = to_spectrum(blocks[: 2 * own], first_ref, twiddle_ref, forward_ref)
    spec_ref[...] = spectrum
    cross = None
    for j in range(own):
        term = times_conj(
            spectrum[(own + j) * parts : (own + j + 1) * parts],
            spectrum[j * parts : (j + 1) * parts],
        )
        cross = term if cross is None else cross + term
    grad_taps = from_spectrum(cross, last_ref, twiddle_ref, inverse_ref)
    for which, block in enumerate((blocks[2 * own], grad_taps)):
        count = parts // groups
        pieces = lane_blocks([block[a * count : (a + 1) * count] for a in range(groups)])
        for g in range(groups):
            out_ref[g, which * count : (which + 1) * count, :] = pieces[members[g]]


def fields_kernel(
    sizes, members, tap_scale, spec_ref, side_ref, first_ref, twiddle_ref, forward_ref, inverse_ref, last_ref, out_ref
):
    parts, channels, own, groups = sizes
    rows = 2 * own + 1
    count = parts // groups
    taps, grad_taps = (
        jnp.concatenate(
            lane_blocks(
                [
                    side_ref[members.index(g), which * count : (which + 1) * count, :]
                    for g in range(groups)
                ]
            ),
            axis=0,
        )
        for which in range(2)
    )
    out_ref[pl.ds(2 * own, parts, stride=rows), :] = grad_taps * tap_scale
    taps = to_spectrum([taps * tap_scale], first_ref, twiddle_ref, forward_ref)
    products = []
    for j in range(own):
        products.append(times(spec_ref[j * parts : (j + 1) * parts, :], taps))
    for j in range(own, 2 * own):
        products.append(times_conj(spec_ref[j * parts : (j + 1) * parts, :], taps))
    fields = from_spectrum(jnp.concatenate(products, axis=0), last_ref, twiddle_ref, inverse_ref)
    width = fields.shape[1] // (2 * own)
    for r in range(2 * own):
        out_ref[pl.ds(r, parts, stride=rows), :] = fields[:, r * width : (r + 1) * width]


def outputs_kernel(
    sizes,
    y_ref,
    query_ref,
    key_ref,
    value_ref,
    upstream_ref,
    mixed_ref,
    grad_query_ref,
    grad_key_ref,
    grad_value_ref,
    grad_filters_ref,
    rows_ref,
):
    parts, channels, own, groups = sizes
    rows = 2 * own + 1
    filter_count = grad_filters_ref.shape[1] // groups
    share = parts // filter_count
    for which in range(2):
        for j in range(own):
            rows_ref[which, pl.ds(j, parts, stride=own), :] = y_ref[
                pl.ds(which * own + j, parts, stride=rows), :
            ]
    mixed_field = rows_ref[0]
    grad_signal = rows_ref[1]
    mixed_ref[...] = (query_ref[...].astype(f32) * mixed_field).astype(bf16)
    grad_query_ref[...] = (upstream_ref[...].astype(f32) * mixed_field).astype(bf16)
    grad_key_ref[...] = (grad_signal * value_ref[...].astype(f32)).astype(bf16)
    grad_value_ref[...] = (grad_signal * key_ref[...].astype(f32)).astype(bf16)
    side = None
    for i in range(share):
        term = y_ref[pl.ds(2 * own + rows * i, filter_count, stride=rows * share), :]
        side = term if side is None else side + term
    block = side.shape[1] // groups
    grad_filters_ref[...] = jnp.concatenate(
        [side[:, g * block : (g + 1) * block] for g in range(groups)], axis=0
    ).T


def call(kernel, out_shape, scratch=(), grant=32, **specs):
    return pl.pallas_call(
        kernel,
        out_shape=out_shape,
        out_specs=jax.tree.map(lambda _: vmem, out_shape),
        scratch_shapes=scratch,
        **specs,
        compiler_params=pltpu.CompilerParams(vmem_limit_bytes=grant * 1024 * 1024),
    )


def shards(gate_query, gate_key, gate_value, filters, upstream):
    channels, width = gate_value.shape
    parts = lax.axis_size("seq")
    groups = lax.axis_size("ch")
    own = channels // parts
    rows = 2 * own + 1
    sizes = (parts, channels, own, groups)
    tap_scale = 1.0 / math.sqrt(parts * width)
    members = [(i + 5) % groups for i in range(groups)]
    order = [16 * ((i + 2) % 4) + (i // 4 + 11) % 16 for i in range(parts)]
    tables = make_tables(parts, width, order)
    first, twiddle, forward, inverse, last = (
        jnp.asarray(tables[name]) for name in ("first", "twiddle", "forward", "inverse", "last")
    )

    def exchange(block):
        block = block.reshape(parts, rows, 1, width)
        block = lax.all_to_all(
            block, "seq", split_axis=0, concat_axis=0, tiled=True, axis_index_groups=[order]
        )
        return block.reshape(parts * rows, width)

    shape = jax.ShapeDtypeStruct
    signal = gate_key.astype(f32) * gate_value.astype(f32)
    grad_gate = upstream.astype(f32) * gate_query.astype(f32)
    packed = call(functools.partial(gates_kernel, sizes), shape((parts * rows, width), f32))(
        signal, grad_gate, filters.T
    )
    packed = exchange(packed)
    spectra, side = call(
        functools.partial(spectra_kernel, sizes, members),
        (
            shape((2 * own * parts, 2 * width), f32),
            shape((groups, 2 * parts // groups, width), f32),
        ),
    )(packed, first, twiddle, forward, inverse, last)
    side = lax.all_to_all(
        side, "ch", split_axis=0, concat_axis=0, tiled=True, axis_index_groups=[members]
    )
    packed = call(functools.partial(fields_kernel, sizes, members, tap_scale), shape((parts * rows, width), f32))(
        spectra, side, first, twiddle, forward, inverse, last
    )
    packed = exchange(packed)
    gates = shape((channels, width), bf16)
    *grads, grad_filters = call(
        functools.partial(outputs_kernel, sizes),
        (gates, gates, gates, gates, shape(filters.shape[::-1], f32)),
        [pltpu.VMEM((2, channels, width), f32)],
    )(packed, gate_query, gate_key, gate_value, upstream)
    return (*grads, grad_filters.T)


def solution(mesh):
    in_specs = (
        P("ch", "seq"),
        P("ch", "seq"),
        P("ch", "seq"),
        P(None, ("seq", "ch")),
        P("ch", "seq"),
    )
    out_specs = (
        P("ch", "seq"),
        P("ch", "seq"),
        P("ch", "seq"),
        P("ch", "seq"),
        P(None, ("seq", "ch")),
    )
    return jax.shard_map(shards, mesh=mesh, in_specs=in_specs, out_specs=out_specs, check_vma=False)
```

```python
import functools
import math

import jax
import jax.numpy as jnp
import ml_dtypes
import numpy as np
from jax import lax
from jax.experimental import pallas as pl
from jax.experimental.pallas import tpu as pltpu
from jax.sharding import PartitionSpec as P

f32 = jnp.float32
bf16 = jnp.bfloat16
vmem = pl.BlockSpec(memory_space=pltpu.VMEM)


def halves(table):
    high = table.astype(ml_dtypes.bfloat16)
    low = (table - high.astype(np.float64)).astype(ml_dtypes.bfloat16)
    return high, low


def make_tables(parts, width, order):
    total = parts * width
    k1 = np.arange(parts) + 0.25
    p = np.asarray(order)
    b = np.arange(width)
    outer = 2.0 * np.pi / parts * (k1[:, None] * p[None, :])
    first = np.concatenate([np.cos(outer), -np.sin(outer)], axis=0)
    last = np.concatenate([np.cos(outer.T), -np.sin(outer.T)], axis=1) / total
    turn = 2.0 * np.pi / total * (k1[:, None] * b[None, :])
    twiddle = np.concatenate([np.cos(turn), -np.sin(turn)], axis=1).astype(np.float32)
    inner = 2.0 * np.pi / width * (b[:, None] * b[None, :] % width)
    cosine, sine = np.cos(inner), np.sin(inner)
    forward = np.block([[cosine, -sine], [sine, cosine]])
    inverse = np.block([[cosine, sine], [-sine, cosine]])
    first_high, first_low = halves(first)
    last_high, last_low = halves(last)
    return dict(
        first=np.concatenate([first_high, first_high, first_low], axis=1),
        last=np.concatenate([last_high, last_high, last_low], axis=1),
        twiddle=twiddle,
        forward=np.stack(halves(forward)),
        inverse=np.stack(halves(inverse)),
    )


def split(value):
    high = value.astype(bf16)
    return high, (value - high.astype(f32)).astype(bf16)


def dot(left, right):
    return jnp.dot(left, right, preferred_element_type=f32)


def stacked_dot(table, value):
    high, low = split(value)
    return dot(table, jnp.concatenate([high, low, high], axis=0))


def table_dot(value, table_ref):
    high, low = split(value)
    return dot(high, table_ref[0]) + (dot(low, table_ref[0]) + dot(high, table_ref[1]))


def to_spectrum(rows, first_ref, twiddle_ref, forward_ref):
    parts, width = rows[0].shape
    stage = stacked_dot(first_ref[...], jnp.concatenate(rows, axis=1))
    cosine, sine = twiddle_ref[:, :width], twiddle_ref[:, width:]
    turned = []
    for r in range(len(rows)):
        real = stage[:parts, r * width : (r + 1) * width]
        imag = stage[parts:, r * width : (r + 1) * width]
        turned.append(
            jnp.concatenate([real * cosine - imag * sine, real * sine + imag * cosine], axis=1)
        )
    return table_dot(jnp.concatenate(turned, axis=0), forward_ref)


def from_spectrum(spectrum, last_ref, twiddle_ref, inverse_ref):
    parts = last_ref.shape[0]
    width = spectrum.shape[1] // 2
    stage = table_dot(spectrum, inverse_ref)
    cosine, sine = twiddle_ref[:, :width], twiddle_ref[:, width:]
    turned = []
    for r in range(stage.shape[0] // parts):
        real = stage[r * parts : (r + 1) * parts, :width]
        imag = stage[r * parts : (r + 1) * parts, width:]
        turned.append(
            jnp.concatenate([real * cosine + imag * sine, imag * cosine - real * sine], axis=0)
        )
    return stacked_dot(last_ref[...], jnp.concatenate(turned, axis=1))


def times(a, b):
    w = a.shape[1] // 2
    ar, ai, br, bi = a[:, :w], a[:, w:], b[:, :w], b[:, w:]
    return jnp.concatenate([ar * br - ai * bi, ar * bi + ai * br], axis=1)


def times_conj(a, b):
    w = a.shape[1] // 2
    ar, ai, br, bi = a[:, :w], a[:, w:], b[:, :w], b[:, w:]
    return jnp.concatenate([ar * br + ai * bi, ai * br - ar * bi], axis=1)


def lane_blocks(pieces):
    count = len(pieces)
    block = pieces[0].shape[1] // count
    lane = lax.broadcasted_iota(jnp.int32, pieces[0].shape, 1) // block
    out = []
    for c in range(count):
        total = pieces[0] if c == 0 else pltpu.roll(pieces[0], (-c) % count * block, 1)
        for a in range(1, count):
            shift = (a - c) % count * block
            moved = pieces[a] if shift == 0 else pltpu.roll(pieces[a], shift, 1)
            total = jnp.where(lane == a, moved, total)
        out.append(total)
    return out


def gates_kernel(sizes, signal_ref, grad_ref, filters_ref, out_ref):
    parts, channels, own, groups = sizes
    rows = 2 * own + 1
    filter_count = filters_ref.shape[1] // groups
    share = parts // filter_count
    for which, source in enumerate((signal_ref, grad_ref)):
        for j in range(own):
            out_ref[pl.ds(which * own + j, parts, stride=rows), :] = source[
                pl.ds(j, parts, stride=own), :
            ]
    taps = filters_ref[...].T
    side = jnp.concatenate(
        [taps[g * filter_count : (g + 1) * filter_count, :] for g in range(groups)], axis=1
    )
    for i in range(share):
        out_ref[pl.ds(2 * own + rows * i, filter_count, stride=rows * share), :] = side


def spectra_kernel(
    sizes, members, x_ref, first_ref, twiddle_ref, forward_ref, inverse_ref, last_ref, spec_ref, out_ref
):
    parts, channels, own, groups = sizes
    rows = 2 * own + 1
    blocks = [x_ref[pl.ds(r, parts, stride=rows), :] for r in range(rows)]
    spectrum = to_spectrum(blocks[: 2 * own], first_ref, twiddle_ref, forward_ref)
    spec_ref[...] = spectrum
    cross = None
    for j in range(own):
        term = times_conj(
            spectrum[(own + j) * parts : (own + j + 1) * parts],
            spectrum[j * parts : (j + 1) * parts],
        )
        cross = term if cross is None else cross + term
    grad_taps = from_spectrum(cross, last_ref, twiddle_ref, inverse_ref)
    for which, block in enumerate((blocks[2 * own], grad_taps)):
        count = parts // groups
        pieces = lane_blocks([block[a * count : (a + 1) * count] for a in range(groups)])
        for g in range(groups):
            out_ref[g, which * count : (which + 1) * count, :] = pieces[members[g]]


def fields_kernel(
    sizes, members, tap_scale, spec_ref, side_ref, first_ref, twiddle_ref, forward_ref, inverse_ref, last_ref, out_ref
):
    parts, channels, own, groups = sizes
    rows = 2 * own + 1
    count = parts // groups
    taps, grad_taps = (
        jnp.concatenate(
            lane_blocks(
                [
                    side_ref[members.index(g), which * count : (which + 1) * count, :]
                    for g in range(groups)
                ]
            ),
            axis=0,
        )
        for which in range(2)
    )
    out_ref[pl.ds(2 * own, parts, stride=rows), :] = grad_taps * tap_scale
    taps = to_spectrum([taps * tap_scale], first_ref, twiddle_ref, forward_ref)
    products = []
    for j in range(own):
        products.append(times(spec_ref[j * parts : (j + 1) * parts, :], taps))
    for j in range(own, 2 * own):
        products.append(times_conj(spec_ref[j * parts : (j + 1) * parts, :], taps))
    fields = from_spectrum(jnp.concatenate(products, axis=0), last_ref, twiddle_ref, inverse_ref)
    width = fields.shape[1] // (2 * own)
    for r in range(2 * own):
        out_ref[pl.ds(r, parts, stride=rows), :] = fields[:, r * width : (r + 1) * width]


def outputs_kernel(
    sizes,
    y_ref,
    query_ref,
    key_ref,
    value_ref,
    upstream_ref,
    mixed_ref,
    grad_query_ref,
    grad_key_ref,
    grad_value_ref,
    grad_filters_ref,
    rows_ref,
):
    parts, channels, own, groups = sizes
    rows = 2 * own + 1
    filter_count = grad_filters_ref.shape[1] // groups
    share = parts // filter_count
    for which in range(2):
        for j in range(own):
            rows_ref[which, pl.ds(j, parts, stride=own), :] = y_ref[
                pl.ds(which * own + j, parts, stride=rows), :
            ]
    mixed_field = rows_ref[0]
    grad_signal = rows_ref[1]
    mixed_ref[...] = (query_ref[...].astype(f32) * mixed_field).astype(bf16)
    grad_query_ref[...] = (upstream_ref[...].astype(f32) * mixed_field).astype(bf16)
    grad_key_ref[...] = (grad_signal * value_ref[...].astype(f32)).astype(bf16)
    grad_value_ref[...] = (grad_signal * key_ref[...].astype(f32)).astype(bf16)
    side = None
    for i in range(share):
        term = y_ref[pl.ds(2 * own + rows * i, filter_count, stride=rows * share), :]
        side = term if side is None else side + term
    block = side.shape[1] // groups
    grad_filters_ref[...] = jnp.concatenate(
        [side[:, g * block : (g + 1) * block] for g in range(groups)], axis=0
    ).T


def call(kernel, out_shape, scratch=(), grant=32, **specs):
    return pl.pallas_call(
        kernel,
        out_shape=out_shape,
        out_specs=jax.tree.map(lambda _: vmem, out_shape),
        scratch_shapes=scratch,
        **specs,
        compiler_params=pltpu.CompilerParams(vmem_limit_bytes=grant * 1024 * 1024),
    )


def shards(gate_query, gate_key, gate_value, filters, upstream):
    channels, width = gate_value.shape
    parts = lax.axis_size("seq")
    groups = lax.axis_size("ch")
    own = channels // parts
    rows = 2 * own + 1
    sizes = (parts, channels, own, groups)
    tap_scale = 1.0 / math.sqrt(parts * width)
    members = [(i + 5) % groups for i in range(groups)]
    order = [16 * ((i + 2) % 4) + (11 - i // 4) % 16 for i in range(parts)]
    tables = make_tables(parts, width, order)
    first, twiddle, forward, inverse, last = (
        jnp.asarray(tables[name]) for name in ("first", "twiddle", "forward", "inverse", "last")
    )

    def exchange(block):
        block = block.reshape(parts, rows, 1, width)
        block = lax.all_to_all(
            block, "seq", split_axis=0, concat_axis=0, tiled=True, axis_index_groups=[order]
        )
        return block.reshape(parts * rows, width)

    shape = jax.ShapeDtypeStruct
    signal = gate_key.astype(f32) * gate_value.astype(f32)
    grad_gate = upstream.astype(f32) * gate_query.astype(f32)
    packed = call(functools.partial(gates_kernel, sizes), shape((parts * rows, width), f32))(
        signal, grad_gate, filters.T
    )
    packed = exchange(packed)
    spectra, side = call(
        functools.partial(spectra_kernel, sizes, members),
        (
            shape((2 * own * parts, 2 * width), f32),
            shape((groups, 2 * parts // groups, width), f32),
        ),
    )(packed, first, twiddle, forward, inverse, last)
    side = lax.all_to_all(
        side, "ch", split_axis=0, concat_axis=0, tiled=True, axis_index_groups=[members]
    )
    packed = call(functools.partial(fields_kernel, sizes, members, tap_scale), shape((parts * rows, width), f32))(
        spectra, side, first, twiddle, forward, inverse, last
    )
    packed = exchange(packed)
    gates = shape((channels, width), bf16)
    *grads, grad_filters = call(
        functools.partial(outputs_kernel, sizes),
        (gates, gates, gates, gates, shape(filters.shape[::-1], f32)),
        [pltpu.VMEM((2, channels, width), f32)],
    )(packed, gate_query, gate_key, gate_value, upstream)
    return (*grads, grad_filters.T)


def solution(mesh):
    in_specs = (
        P("ch", "seq"),
        P("ch", "seq"),
        P("ch", "seq"),
        P(None, ("seq", "ch")),
        P("ch", "seq"),
    )
    out_specs = (
        P("ch", "seq"),
        P("ch", "seq"),
        P("ch", "seq"),
        P("ch", "seq"),
        P(None, ("seq", "ch")),
    )
    return jax.shard_map(shards, mesh=mesh, in_specs=in_specs, out_specs=out_specs, check_vma=False)
```

```python
import functools
import math

import jax
import jax.numpy as jnp
import ml_dtypes
import numpy as np
from jax import lax
from jax.experimental import pallas as pl
from jax.experimental.pallas import tpu as pltpu
from jax.sharding import PartitionSpec as P

f32 = jnp.float32
bf16 = jnp.bfloat16
vmem = pl.BlockSpec(memory_space=pltpu.VMEM)


def halves(table):
    high = table.astype(ml_dtypes.bfloat16)
    low = (table - high.astype(np.float64)).astype(ml_dtypes.bfloat16)
    return high, low


def make_tables(parts, width, order):
    total = parts * width
    k1 = np.arange(parts) + 0.25
    p = np.asarray(order)
    b = np.arange(width)
    outer = 2.0 * np.pi / parts * (k1[:, None] * p[None, :])
    first = np.concatenate([np.cos(outer), -np.sin(outer)], axis=0)
    last = np.concatenate([np.cos(outer.T), -np.sin(outer.T)], axis=1) / total
    turn = 2.0 * np.pi / total * (k1[:, None] * b[None, :])
    twiddle = np.concatenate([np.cos(turn), -np.sin(turn)], axis=1).astype(np.float32)
    inner = 2.0 * np.pi / width * (b[:, None] * b[None, :] % width)
    cosine, sine = np.cos(inner), np.sin(inner)
    forward = np.block([[cosine, -sine], [sine, cosine]])
    inverse = np.block([[cosine, sine], [-sine, cosine]])
    first_high, first_low = halves(first)
    last_high, last_low = halves(last)
    return dict(
        first=np.concatenate([first_high, first_high, first_low], axis=1),
        last=np.concatenate([last_high, last_high, last_low], axis=1),
        twiddle=twiddle,
        forward=np.stack(halves(forward)),
        inverse=np.stack(halves(inverse)),
    )


def split(value):
    high = value.astype(bf16)
    return high, (value - high.astype(f32)).astype(bf16)


def dot(left, right):
    return jnp.dot(left, right, preferred_element_type=f32)


def stacked_dot(table, value):
    high, low = split(value)
    return dot(table, jnp.concatenate([high, low, high], axis=0))


def table_dot(value, table_ref):
    high, low = split(value)
    return dot(high, table_ref[0]) + (dot(low, table_ref[0]) + dot(high, table_ref[1]))


def to_spectrum(rows, first_ref, twiddle_ref, forward_ref):
    parts, width = rows[0].shape
    stage = stacked_dot(first_ref[...], jnp.concatenate(rows, axis=1))
    cosine, sine = twiddle_ref[:, :width], twiddle_ref[:, width:]
    turned = []
    for r in range(len(rows)):
        real = stage[:parts, r * width : (r + 1) * width]
        imag = stage[parts:, r * width : (r + 1) * width]
        turned.append(
            jnp.concatenate([real * cosine - imag * sine, real * sine + imag * cosine], axis=1)
        )
    return table_dot(jnp.concatenate(turned, axis=0), forward_ref)


def from_spectrum(spectrum, last_ref, twiddle_ref, inverse_ref):
    parts = last_ref.shape[0]
    width = spectrum.shape[1] // 2
    stage = table_dot(spectrum, inverse_ref)
    cosine, sine = twiddle_ref[:, :width], twiddle_ref[:, width:]
    turned = []
    for r in range(stage.shape[0] // parts):
        real = stage[r * parts : (r + 1) * parts, :width]
        imag = stage[r * parts : (r + 1) * parts, width:]
        turned.append(
            jnp.concatenate([real * cosine + imag * sine, imag * cosine - real * sine], axis=0)
        )
    return stacked_dot(last_ref[...], jnp.concatenate(turned, axis=1))


def times(a, b):
    w = a.shape[1] // 2
    ar, ai, br, bi = a[:, :w], a[:, w:], b[:, :w], b[:, w:]
    return jnp.concatenate([ar * br - ai * bi, ar * bi + ai * br], axis=1)


def times_conj(a, b):
    w = a.shape[1] // 2
    ar, ai, br, bi = a[:, :w], a[:, w:], b[:, :w], b[:, w:]
    return jnp.concatenate([ar * br + ai * bi, ai * br - ar * bi], axis=1)


def lane_blocks(pieces):
    count = len(pieces)
    block = pieces[0].shape[1] // count
    lane = lax.broadcasted_iota(jnp.int32, pieces[0].shape, 1) // block
    pieces = list(pieces)
    half = count // 2
    while half:
        upper = lane // half % 2 == 1
        for a in range(count):
            if a // half % 2 == 0:
                low, high = pieces[a], pieces[a + half]
                pieces[a] = jnp.where(upper, pltpu.roll(high, half * block, 1), low)
                pieces[a + half] = jnp.where(upper, high, pltpu.roll(low, (count - half) * block, 1))
        half //= 2
    return pieces


def gates_kernel(sizes, signal_ref, grad_ref, filters_ref, out_ref):
    parts, channels, own, groups = sizes
    rows = 2 * own + 1
    filter_count = filters_ref.shape[1] // groups
    share = parts // filter_count
    for which, source in enumerate((signal_ref, grad_ref)):
        for j in range(own):
            out_ref[pl.ds(which * own + j, parts, stride=rows), :] = source[
                pl.ds(j, parts, stride=own), :
            ]
    taps = filters_ref[...].T
    side = jnp.concatenate(
        [taps[g * filter_count : (g + 1) * filter_count, :] for g in range(groups)], axis=1
    )
    for i in range(share):
        out_ref[pl.ds(2 * own + rows * i, filter_count, stride=rows * share), :] = side


def spectra_kernel(
    sizes, members, x_ref, first_ref, twiddle_ref, forward_ref, inverse_ref, last_ref, spec_ref, out_ref
):
    parts, channels, own, groups = sizes
    rows = 2 * own + 1
    blocks = [x_ref[pl.ds(r, parts, stride=rows), :] for r in range(rows)]
    spectrum = to_spectrum(blocks[: 2 * own], first_ref, twiddle_ref, forward_ref)
    spec_ref[...] = spectrum
    cross = None
    for j in range(own):
        term = times_conj(
            spectrum[(own + j) * parts : (own + j + 1) * parts],
            spectrum[j * parts : (j + 1) * parts],
        )
        cross = term if cross is None else cross + term
    grad_taps = from_spectrum(cross, last_ref, twiddle_ref, inverse_ref)
    for which, block in enumerate((blocks[2 * own], grad_taps)):
        count = parts // groups
        pieces = lane_blocks([block[a * count : (a + 1) * count] for a in range(groups)])
        for g in range(groups):
            out_ref[g, which * count : (which + 1) * count, :] = pieces[members[g]]


def fields_kernel(
    sizes, members, tap_scale, spec_ref, side_ref, first_ref, twiddle_ref, forward_ref, inverse_ref, last_ref, out_ref
):
    parts, channels, own, groups = sizes
    rows = 2 * own + 1
    count = parts // groups
    taps, grad_taps = (
        jnp.concatenate(
            lane_blocks(
                [
                    side_ref[members.index(g), which * count : (which + 1) * count, :]
                    for g in range(groups)
                ]
            ),
            axis=0,
        )
        for which in range(2)
    )
    out_ref[pl.ds(2 * own, parts, stride=rows), :] = grad_taps * tap_scale
    taps = to_spectrum([taps * tap_scale], first_ref, twiddle_ref, forward_ref)
    products = []
    for j in range(own):
        products.append(times(spec_ref[j * parts : (j + 1) * parts, :], taps))
    for j in range(own, 2 * own):
        products.append(times_conj(spec_ref[j * parts : (j + 1) * parts, :], taps))
    fields = from_spectrum(jnp.concatenate(products, axis=0), last_ref, twiddle_ref, inverse_ref)
    width = fields.shape[1] // (2 * own)
    for r in range(2 * own):
        out_ref[pl.ds(r, parts, stride=rows), :] = fields[:, r * width : (r + 1) * width]


def outputs_kernel(
    sizes,
    y_ref,
    query_ref,
    key_ref,
    value_ref,
    upstream_ref,
    mixed_ref,
    grad_query_ref,
    grad_key_ref,
    grad_value_ref,
    grad_filters_ref,
    rows_ref,
):
    parts, channels, own, groups = sizes
    rows = 2 * own + 1
    filter_count = grad_filters_ref.shape[1] // groups
    share = parts // filter_count
    for which in range(2):
        for j in range(own):
            rows_ref[which, pl.ds(j, parts, stride=own), :] = y_ref[
                pl.ds(which * own + j, parts, stride=rows), :
            ]
    mixed_field = rows_ref[0]
    grad_signal = rows_ref[1]
    mixed_ref[...] = (query_ref[...].astype(f32) * mixed_field).astype(bf16)
    grad_query_ref[...] = (upstream_ref[...].astype(f32) * mixed_field).astype(bf16)
    grad_key_ref[...] = (grad_signal * value_ref[...].astype(f32)).astype(bf16)
    grad_value_ref[...] = (grad_signal * key_ref[...].astype(f32)).astype(bf16)
    side = None
    for i in range(share):
        term = y_ref[pl.ds(2 * own + rows * i, filter_count, stride=rows * share), :]
        side = term if side is None else side + term
    block = side.shape[1] // groups
    grad_filters_ref[...] = jnp.concatenate(
        [side[:, g * block : (g + 1) * block] for g in range(groups)], axis=0
    ).T


def call(kernel, out_shape, scratch=(), grant=32, **specs):
    return pl.pallas_call(
        kernel,
        out_shape=out_shape,
        out_specs=jax.tree.map(lambda _: vmem, out_shape),
        scratch_shapes=scratch,
        **specs,
        compiler_params=pltpu.CompilerParams(vmem_limit_bytes=grant * 1024 * 1024),
    )


def shards(gate_query, gate_key, gate_value, filters, upstream):
    channels, width = gate_value.shape
    parts = lax.axis_size("seq")
    groups = lax.axis_size("ch")
    own = channels // parts
    rows = 2 * own + 1
    sizes = (parts, channels, own, groups)
    tap_scale = 1.0 / math.sqrt(parts * width)
    members = [(i + 5) % groups for i in range(groups)]
    order = [16 * ((i + 2) % 4) + (i // 4 + 11) % 16 for i in range(parts)]
    tables = make_tables(parts, width, order)
    first, twiddle, forward, inverse, last = (
        jnp.asarray(tables[name]) for name in ("first", "twiddle", "forward", "inverse", "last")
    )

    def exchange(block):
        block = block.reshape(parts, rows, 1, width)
        block = lax.all_to_all(
            block, "seq", split_axis=0, concat_axis=0, tiled=True, axis_index_groups=[order]
        )
        return block.reshape(parts * rows, width)

    shape = jax.ShapeDtypeStruct
    signal = gate_key.astype(f32) * gate_value.astype(f32)
    grad_gate = upstream.astype(f32) * gate_query.astype(f32)
    packed = call(functools.partial(gates_kernel, sizes), shape((parts * rows, width), f32))(
        signal, grad_gate, filters.T
    )
    packed = exchange(packed)
    spectra, side = call(
        functools.partial(spectra_kernel, sizes, members),
        (
            shape((2 * own * parts, 2 * width), f32),
            shape((groups, 2 * parts // groups, width), f32),
        ),
    )(packed, first, twiddle, forward, inverse, last)
    side = lax.all_to_all(
        side, "ch", split_axis=0, concat_axis=0, tiled=True, axis_index_groups=[members]
    )
    packed = call(functools.partial(fields_kernel, sizes, members, tap_scale), shape((parts * rows, width), f32))(
        spectra, side, first, twiddle, forward, inverse, last
    )
    packed = exchange(packed)
    gates = shape((channels, width), bf16)
    *grads, grad_filters = call(
        functools.partial(outputs_kernel, sizes),
        (gates, gates, gates, gates, shape(filters.shape[::-1], f32)),
        [pltpu.VMEM((2, channels, width), f32)],
    )(packed, gate_query, gate_key, gate_value, upstream)
    return (*grads, grad_filters.T)


def solution(mesh):
    in_specs = (
        P("ch", "seq"),
        P("ch", "seq"),
        P("ch", "seq"),
        P(None, ("seq", "ch")),
        P("ch", "seq"),
    )
    out_specs = (
        P("ch", "seq"),
        P("ch", "seq"),
        P("ch", "seq"),
        P("ch", "seq"),
        P(None, ("seq", "ch")),
    )
    return jax.shard_map(shards, mesh=mesh, in_specs=in_specs, out_specs=out_specs, check_vma=False)
```

```python
import functools
import math

import jax
import jax.numpy as jnp
import ml_dtypes
import numpy as np
from jax import lax
from jax.experimental import pallas as pl
from jax.experimental.pallas import tpu as pltpu
from jax.sharding import PartitionSpec as P

f32 = jnp.float32
bf16 = jnp.bfloat16
vmem = pl.BlockSpec(memory_space=pltpu.VMEM)


def halves(table):
    high = table.astype(ml_dtypes.bfloat16)
    low = (table - high.astype(np.float64)).astype(ml_dtypes.bfloat16)
    return high, low


def make_tables(parts, width, order):
    total = parts * width
    k1 = np.arange(parts) + 0.25
    p = np.asarray(order)
    b = np.arange(width)
    outer = 2.0 * np.pi / parts * (k1[:, None] * p[None, :])
    first = np.concatenate([np.cos(outer), -np.sin(outer)], axis=0)
    last = np.concatenate([np.cos(outer.T), -np.sin(outer.T)], axis=1) / total
    turn = 2.0 * np.pi / total * (k1[:, None] * b[None, :])
    twiddle = np.concatenate([np.cos(turn), -np.sin(turn)], axis=1).astype(np.float32)
    inner = 2.0 * np.pi / width * (b[:, None] * b[None, :] % width)
    cosine, sine = np.cos(inner), np.sin(inner)
    forward = np.block([[cosine, -sine], [sine, cosine]])
    inverse = np.block([[cosine, sine], [-sine, cosine]])
    first_high, first_low = halves(first)
    last_high, last_low = halves(last)
    return dict(
        first=np.concatenate([first_high, first_high, first_low], axis=1),
        last=np.concatenate([last_high, last_high, last_low], axis=1),
        twiddle=twiddle,
        forward=np.stack(halves(forward)),
        inverse=np.stack(halves(inverse)),
    )


def split(value):
    high = value.astype(bf16)
    return high, (value - high.astype(f32)).astype(bf16)


def dot(left, right):
    return jnp.dot(left, right, preferred_element_type=f32)


def stacked_dot(table, value):
    high, low = split(value)
    return dot(table, jnp.concatenate([high, low, high], axis=0))


def table_dot(value, table_ref):
    high, low = split(value)
    return dot(high, table_ref[0]) + (dot(low, table_ref[0]) + dot(high, table_ref[1]))


def to_spectrum(rows, first_ref, twiddle_ref, forward_ref):
    parts, width = rows[0].shape
    stage = stacked_dot(first_ref[...], jnp.concatenate(rows, axis=1))
    cosine, sine = twiddle_ref[:, :width], twiddle_ref[:, width:]
    turned = []
    for r in range(len(rows)):
        real = stage[:parts, r * width : (r + 1) * width]
        imag = stage[parts:, r * width : (r + 1) * width]
        turned.append(
            jnp.concatenate([real * cosine - imag * sine, real * sine + imag * cosine], axis=1)
        )
    return table_dot(jnp.concatenate(turned, axis=0), forward_ref)


def from_spectrum(spectrum, last_ref, twiddle_ref, inverse_ref):
    parts = last_ref.shape[0]
    width = spectrum.shape[1] // 2
    stage = table_dot(spectrum, inverse_ref)
    cosine, sine = twiddle_ref[:, :width], twiddle_ref[:, width:]
    turned = []
    for r in range(stage.shape[0] // parts):
        real = stage[r * parts : (r + 1) * parts, :width]
        imag = stage[r * parts : (r + 1) * parts, width:]
        turned.append(
            jnp.concatenate([real * cosine + imag * sine, imag * cosine - real * sine], axis=0)
        )
    return stacked_dot(last_ref[...], jnp.concatenate(turned, axis=1))


def times(a, b):
    w = a.shape[1] // 2
    ar, ai, br, bi = a[:, :w], a[:, w:], b[:, :w], b[:, w:]
    return jnp.concatenate([ar * br - ai * bi, ar * bi + ai * br], axis=1)


def times_conj(a, b):
    w = a.shape[1] // 2
    ar, ai, br, bi = a[:, :w], a[:, w:], b[:, :w], b[:, w:]
    return jnp.concatenate([ar * br + ai * bi, ai * br - ar * bi], axis=1)


def lane_blocks(pieces):
    count = len(pieces)
    block = pieces[0].shape[1] // count
    lane = lax.broadcasted_iota(jnp.int32, pieces[0].shape, 1) // block
    out = []
    for c in range(count):
        total = pieces[0] if c == 0 else pltpu.roll(pieces[0], (-c) % count * block, 1)
        for a in range(1, count):
            shift = (a - c) % count * block
            moved = pieces[a] if shift == 0 else pltpu.roll(pieces[a], shift, 1)
            total = jnp.where(lane == a, moved, total)
        out.append(total)
    return out


def gates_kernel(sizes, signal_ref, grad_ref, filters_ref, out_ref):
    parts, channels, own, groups = sizes
    rows = 2 * own + 1
    filter_count = filters_ref.shape[1] // groups
    share = parts // filter_count
    for which, source in enumerate((signal_ref, grad_ref)):
        for j in range(own):
            out_ref[pl.ds(which * own + j, parts, stride=rows), :] = source[
                pl.ds(j, parts, stride=own), :
            ]
    taps = filters_ref[...].T
    side = jnp.concatenate(
        [taps[g * filter_count : (g + 1) * filter_count, :] for g in range(groups)], axis=1
    )
    for i in range(share):
        out_ref[pl.ds(2 * own + rows * i, filter_count, stride=rows * share), :] = side


def spectra_kernel(
    sizes, members, x_ref, first_ref, twiddle_ref, forward_ref, inverse_ref, last_ref, spec_ref, out_ref
):
    parts, channels, own, groups = sizes
    rows = 2 * own + 1
    blocks = [x_ref[pl.ds(r, parts, stride=rows), :] for r in range(rows)]
    spectrum = to_spectrum(blocks[: 2 * own], first_ref, twiddle_ref, forward_ref)
    spec_ref[...] = spectrum
    cross = None
    for j in range(own):
        term = times_conj(
            spectrum[(own + j) * parts : (own + j + 1) * parts],
            spectrum[j * parts : (j + 1) * parts],
        )
        cross = term if cross is None else cross + term
    grad_taps = from_spectrum(cross, last_ref, twiddle_ref, inverse_ref)
    for which, block in enumerate((blocks[2 * own], grad_taps)):
        count = parts // groups
        pieces = lane_blocks([block[a * count : (a + 1) * count] for a in range(groups)])
        for g in range(groups):
            out_ref[g, which * count : (which + 1) * count, :] = pieces[members[g]]


def fields_kernel(
    sizes, members, tap_scale, spec_ref, side_ref, first_ref, twiddle_ref, forward_ref, inverse_ref, last_ref, out_ref
):
    parts, channels, own, groups = sizes
    rows = 2 * own + 1
    count = parts // groups
    taps, grad_taps = (
        jnp.concatenate(
            lane_blocks(
                [
                    side_ref[members.index(g), which * count : (which + 1) * count, :]
                    for g in range(groups)
                ]
            ),
            axis=0,
        )
        for which in range(2)
    )
    out_ref[pl.ds(2 * own, parts, stride=rows), :] = grad_taps * tap_scale
    taps = to_spectrum([taps * tap_scale], first_ref, twiddle_ref, forward_ref)
    products = []
    for j in range(own):
        products.append(times(spec_ref[j * parts : (j + 1) * parts, :], taps))
    for j in range(own, 2 * own):
        products.append(times_conj(spec_ref[j * parts : (j + 1) * parts, :], taps))
    fields = from_spectrum(jnp.concatenate(products, axis=0), last_ref, twiddle_ref, inverse_ref)
    width = fields.shape[1] // (2 * own)
    for r in range(2 * own):
        out_ref[pl.ds(r, parts, stride=rows), :] = fields[:, r * width : (r + 1) * width]


def outputs_kernel(
    sizes,
    y_ref,
    query_ref,
    key_ref,
    value_ref,
    upstream_ref,
    mixed_ref,
    grad_query_ref,
    grad_key_ref,
    grad_value_ref,
    grad_filters_ref,
    rows_ref,
):
    parts, channels, own, groups = sizes
    rows = 2 * own + 1
    filter_count = grad_filters_ref.shape[1] // groups
    share = parts // filter_count
    for which in range(2):
        for j in range(own):
            rows_ref[which, pl.ds(j, parts, stride=own), :] = y_ref[
                pl.ds(which * own + j, parts, stride=rows), :
            ]
    mixed_field = rows_ref[0]
    grad_signal = rows_ref[1]
    mixed_ref[...] = (query_ref[...].astype(f32) * mixed_field).astype(bf16)
    grad_query_ref[...] = (upstream_ref[...].astype(f32) * mixed_field).astype(bf16)
    grad_key_ref[...] = (grad_signal * value_ref[...].astype(f32)).astype(bf16)
    grad_value_ref[...] = (grad_signal * key_ref[...].astype(f32)).astype(bf16)
    side = None
    for i in range(share):
        term = y_ref[pl.ds(2 * own + rows * i, filter_count, stride=rows * share), :]
        side = term if side is None else side + term
    block = side.shape[1] // groups
    grad_filters_ref[...] = jnp.concatenate(
        [side[:, g * block : (g + 1) * block] for g in range(groups)], axis=0
    ).T


def call(kernel, out_shape, scratch=(), grant=32, **specs):
    return pl.pallas_call(
        kernel,
        out_shape=out_shape,
        out_specs=jax.tree.map(lambda _: vmem, out_shape),
        scratch_shapes=scratch,
        **specs,
        compiler_params=pltpu.CompilerParams(vmem_limit_bytes=grant * 1024 * 1024),
    )


def shards(gate_query, gate_key, gate_value, filters, upstream):
    channels, width = gate_value.shape
    parts = lax.axis_size("seq")
    groups = lax.axis_size("ch")
    own = channels // parts
    rows = 2 * own + 1
    sizes = (parts, channels, own, groups)
    tap_scale = 1.0 / math.sqrt(parts * width)
    members = [(i + 5) % groups for i in range(groups)]
    order = [43] + [i for i in range(parts) if i != 43]
    tables = make_tables(parts, width, order)
    first, twiddle, forward, inverse, last = (
        jnp.asarray(tables[name]) for name in ("first", "twiddle", "forward", "inverse", "last")
    )

    def exchange(block):
        block = block.reshape(parts, rows, 1, width)
        block = lax.all_to_all(
            block, "seq", split_axis=0, concat_axis=0, tiled=True, axis_index_groups=[order]
        )
        return block.reshape(parts * rows, width)

    shape = jax.ShapeDtypeStruct
    signal = gate_key.astype(f32) * gate_value.astype(f32)
    grad_gate = upstream.astype(f32) * gate_query.astype(f32)
    packed = call(functools.partial(gates_kernel, sizes), shape((parts * rows, width), f32))(
        signal, grad_gate, filters.T
    )
    packed = exchange(packed)
    spectra, side = call(
        functools.partial(spectra_kernel, sizes, members),
        (
            shape((2 * own * parts, 2 * width), f32),
            shape((groups, 2 * parts // groups, width), f32),
        ),
    )(packed, first, twiddle, forward, inverse, last)
    side = lax.all_to_all(
        side, "ch", split_axis=0, concat_axis=0, tiled=True, axis_index_groups=[members]
    )
    packed = call(functools.partial(fields_kernel, sizes, members, tap_scale), shape((parts * rows, width), f32))(
        spectra, side, first, twiddle, forward, inverse, last
    )
    packed = exchange(packed)
    gates = shape((channels, width), bf16)
    *grads, grad_filters = call(
        functools.partial(outputs_kernel, sizes),
        (gates, gates, gates, gates, shape(filters.shape[::-1], f32)),
        [pltpu.VMEM((2, channels, width), f32)],
    )(packed, gate_query, gate_key, gate_value, upstream)
    return (*grads, grad_filters.T)


def solution(mesh):
    in_specs = (
        P("ch", "seq"),
        P("ch", "seq"),
        P("ch", "seq"),
        P(None, ("seq", "ch")),
        P("ch", "seq"),
    )
    out_specs = (
        P("ch", "seq"),
        P("ch", "seq"),
        P("ch", "seq"),
        P("ch", "seq"),
        P(None, ("seq", "ch")),
    )
    return jax.shard_map(shards, mesh=mesh, in_specs=in_specs, out_specs=out_specs, check_vma=False)
```
